256 devices in a mesh: band: 8 (over y, core), ka: 32 (over z, x).
Axes of the slice: x: 4, y: 4, z: 8, core: 2. Of those that a mesh axis runs over, the one named last changes fastest.
Arguments:
- transfer: bfloat16 [1024, 2048], P('band', 'ka'), may hold values from -6 to 6
- bessel_table: bfloat16 [1024, 2048, 640], P('band', 'ka'), may hold values from -0.125 to 0.125
- k_weight: float32 [2048], P('ka'), may hold values from 0.5 to 2
- power_spectrum: float32 [2048], P('ka'), may hold values from 0.25 to 4
- radial_weight: float32 [640], replicated, may hold values from 0.2 to 1
- tile_list: int32 [104, 2], P('band'), may hold values from -1 to 7, as said below
Outputs:
- bispectrum: bfloat16 [104, 128, 128, 128], P('band', 'ka')
The draws below stay inside these ranges and needn't reach their ends.
Inputs may be any that keep to these rules, and one draw needn't show every extreme that they name: `tile_list`: each row is a pair (first, second) of l block indices with first <= second, or -1, -1 for an empty slot. Every pair with first <= second < 8 occurs exactly once over all slots. Group g owns rows g * 13 to (g + 1) * 13 - 1; one group's rows are all filled.
All inputs are finite; a program needn't handle non-finite values.
Results may differ from the reference program's by a relative error of at most 0.0077.
Values may be sent and summed in bfloat16 or wider, within the bound.
No kernel may reach another device: no remote copies, remote signals or barrier semaphores. Data moves between devices by JAX's collectives and lax.ppermute only.
A program may use at most 64 MiB of HBM per device.

```python
import math
import jax
import jax.numpy as jnp
import numpy as np
from jax import lax

NB = 8
LB = 128
K = 2048
R = 640
L = 1024
NT = 36
TPG = 13
SLOTS = 104


def draw_tile_list(key, part):
    groups = SLOTS // TPG
    key_order = jax.random.fold_in(key, 11)
    key_busy = jax.random.fold_in(key, 12)
    key_other = jax.random.fold_in(key, 13)
    upper_first, upper_second = np.triu_indices(NB)
    first_table = jnp.asarray(upper_first, jnp.int32)
    second_table = jnp.asarray(upper_second, jnp.int32)
    tile_order = jax.random.permutation(key_order, NT).astype(jnp.int32)
    busiest = jax.random.randint(key_busy, (), 0, groups).astype(jnp.int32)
    other_pick = jax.random.permutation(key_other, (groups - 1) * TPG)[:NT - TPG].astype(jnp.int32)
    other_group = other_pick // TPG
    other_group = other_group + (other_group >= busiest).astype(jnp.int32)
    other_slot = other_group * TPG + other_pick % TPG
    busy_slot = busiest * TPG + jnp.arange(TPG, dtype=jnp.int32)
    slot_tile = jnp.full((SLOTS,), -1, jnp.int32)
    slot_tile = slot_tile.at[busy_slot].set(tile_order[:TPG])
    slot_tile = slot_tile.at[other_slot].set(tile_order[TPG:])
    slot_valid = slot_tile >= 0
    safe_index = jnp.maximum(slot_tile, 0)
    first_block = jnp.where(slot_valid, first_table[safe_index], -1)
    second_block = jnp.where(slot_valid, second_table[safe_index], -1)
    return jnp.stack([first_block, second_block], axis=1).astype(jnp.int32)


def levels(own_key, shape, shards, least, top_value):
    def one(axis_at, shards_of):
        steps = jax.random.uniform(jax.random.fold_in(jax.random.fold_in(own_key, 6), axis_at), (shards_of,), jnp.float32, least / len(shards), top_value / len(shards))
        return jnp.repeat(jnp.exp(steps), shape[axis_at] // shards_of).reshape((-1,) + (1,) * (len(shape) - axis_at - 1))

    loudness = one(*shards[0])
    for cut in shards[1:]:
        loudness = loudness * one(*cut)
    return loudness


def scatter_about(own_key, extent, deviation, most, shards=(), kind=jnp.bfloat16):
    drawn = jax.random.normal(own_key, extent, jnp.float32) * deviation
    if len(shards) > 0:
        drawn = levels(own_key, extent, shards, -0.22, 0.18) * drawn
    return jnp.clip(drawn, min=-most, max=most).astype(kind)


def setup_inputs(seed: int = 0) -> dict:
    key_of = jax.random.split(jax.random.key(seed), 7)
    transfer = scatter_about(key_of[0], (L, K), 1.0, 6.0, ((0, 8), (1, 32)))
    bessel_table = scatter_about(key_of[1], (L, K, R), K ** -0.5, 0.125, ((0, 8), (1, 32)))
    k_weight = jnp.clip(jnp.exp(math.log(2.0) - 1.3862944 * jax.random.uniform(key_of[2], (K,), jnp.float32) ** levels(key_of[2], (K,), ((0, 32),), -0.2, 0.2)), 0.5, 2.0)
    power_spectrum = jnp.clip(jnp.exp(math.log(4.0) - 2.7725887 * jax.random.uniform(key_of[3], (K,), jnp.float32) ** levels(key_of[3], (K,), ((0, 32),), -0.2, 0.2)), 0.25, 4.0)
    radial_weight = jnp.clip(jnp.exp(jax.random.uniform(key_of[4], (R,), jnp.float32, math.log(0.2), math.log(1.0))), 0.2, 1.0)
    tile_list = draw_tile_list(jax.random.fold_in(key_of[6], 71), 0)
    return {"transfer": transfer, "bessel_table": bessel_table, "k_weight": k_weight, "power_spectrum": power_spectrum, "radial_weight": radial_weight, "tile_list": tile_list}


def triangle_mask(l_first, l_second, l_third):
    one = l_first[:, None, None]
    two = l_second[None, :, None]
    three = l_third[None, None, :]
    l_total = one + two + three
    return (l_total % 2 == 0) & (one <= two) & (two <= three) & (three <= one + two)

def tile_values(rows_first, rows_second, slab_table, l_first, l_second, l_third):
    alpha_one = rows_first[:, 0].astype(jnp.float32)
    beta_one = rows_first[:, 1].astype(jnp.float32)
    alpha_two = rows_second[:, 0].astype(jnp.float32)
    beta_two = rows_second[:, 1].astype(jnp.float32)
    mixed_pair = (alpha_one[:, None, :] * beta_two[None] + beta_one[:, None, :] * alpha_two[None]).astype(jnp.bfloat16)
    beta_pair = (beta_one[:, None, :] * beta_two[None]).astype(jnp.bfloat16)
    pair_table = jnp.concatenate([mixed_pair, beta_pair], axis=-1)
    row_count = rows_first.shape[0]
    flat = pair_table.reshape(row_count * rows_second.shape[0], pair_table.shape[-1])
    values = jnp.dot(flat, slab_table.T, preferred_element_type=jnp.float32)
    values = values.reshape(row_count, rows_second.shape[0], slab_table.shape[0])
    keep = triangle_mask(l_first, l_second, l_third)
    return jnp.where(keep, values, 0.0).astype(jnp.bfloat16)

def reference(transfer, bessel_table, k_weight, power_spectrum, radial_weight, tile_list):
    scaled = transfer.astype(jnp.float32) * k_weight[None, :]
    weighted = jnp.stack([scaled, scaled * power_spectrum[None, :]], axis=1).astype(jnp.bfloat16)

    def one_row(row_pair):
        return jnp.dot(row_pair[0], row_pair[1], preferred_element_type=jnp.float32)
    radial = lax.map(one_row, (weighted, bessel_table))
    radial_rounded = radial.astype(jnp.bfloat16)
    slab = radial_rounded[L - LB:].astype(jnp.float32)
    scale_radial = radial_weight * (0.5 / math.sqrt(R))
    slab_table = jnp.concatenate([slab[:, 1] * scale_radial[None, :], slab[:, 0] * scale_radial[None, :]], axis=-1).astype(jnp.bfloat16)
    l_third = (2 + (NB - 1) * LB + jnp.arange(LB)).astype(jnp.int32)

    def one_slot(block_pair):
        first_block = jnp.maximum(block_pair[0], 0).astype(jnp.int32)
        second_block = jnp.maximum(block_pair[1], 0).astype(jnp.int32)

        def filled(unused):
            start_first = (first_block * LB).astype(jnp.int32)
            start_second = (second_block * LB).astype(jnp.int32)
            rows_first = lax.dynamic_slice_in_dim(radial_rounded, start_first, LB, 0)
            rows_second = lax.dynamic_slice_in_dim(radial_rounded, start_second, LB, 0)
            l_first = (2 + start_first + jnp.arange(LB)).astype(jnp.int32)
            l_second = (2 + start_second + jnp.arange(LB)).astype(jnp.int32)
            return tile_values(rows_first, rows_second, slab_table, l_first, l_second, l_third)

        def vacant(unused):
            return jnp.zeros((LB, LB, LB), jnp.bfloat16)
        return lax.cond(block_pair[0] >= 0, filled, vacant, block_pair)
    return lax.map(one_slot, tile_list)
```

```python
import math

import jax
import jax.numpy as jnp
from jax import lax
from jax.experimental import pallas as pl
from jax.experimental.pallas import tpu as pltpu
from jax.sharding import PartitionSpec as P

NB = 8
LB = 128
R = 640
LOW = 3
FULL = NB - LOW
F32 = jnp.float32
BF16 = jnp.bfloat16


def project_kernel(weight_ref, bessel_ref, out_ref):
    dests, rows, depth = weight_ref.shape
    for dest in range(dests):
        per = depth // bessel_ref.shape[1]
        table = bessel_ref[dest * per : (dest + 1) * per].reshape(depth, R)
        out_ref[dest] = jnp.dot(weight_ref[dest], table, preferred_element_type=F32).astype(BF16)


def project(weights, bessel, steps):
    count, rows, depth = weights.shape
    width = bessel.shape[0]
    return pl.pallas_call(
        project_kernel,
        grid=(steps,),
        in_specs=[
            pl.BlockSpec((count // steps, rows, depth), lambda i: (i, 0, 0)),
            pl.BlockSpec((width // steps,) + bessel.shape[1:], lambda i: (i, 0, 0)),
        ],
        out_specs=pl.BlockSpec((count // steps, rows, R), lambda i: (i, 0, 0)),
        out_shape=jax.ShapeDtypeStruct((count, rows, R), BF16),
        compiler_params=pltpu.CompilerParams(vmem_limit_bytes=32 << 20),
        name="project",
    )(weights, bessel)


def tile_kernel(place_ref, tiles_ref, first_ref, own_ref, other_ref, scale_ref, out_ref, first32, full32, slab_t, pair):
    slot = pl.program_id(0)
    core = place_ref[0]
    row_offset = place_ref[1]
    parts, _, width, _ = own_ref.shape

    @pl.when(slot == 0)
    def _():
        first32[...] = first_ref[...].astype(F32)
        for part in range(parts):
            for block in range(FULL):
                where = pl.ds(part * width, width)
                full32[core, block, where, :] = own_ref[part, block].astype(F32)
                full32[1 - core, block, where, :] = other_ref[part, block].astype(F32)
        scale = scale_ref[...]
        slab_t[:R] = (full32[1, FULL - 1] * scale).T.astype(BF16)
        slab_t[R:] = (full32[0, FULL - 1] * scale).T.astype(BF16)

    one = tiles_ref[slot, 0]
    two = tiles_ref[slot, 1]
    live = (one >= 0) & (one + two >= NB - LOW)

    @pl.when(live)
    def _():
        block = two - LOW
        for row in range(width):
            alpha_one = first32[one, pl.ds(row, 1), :]
            beta_one = first32[one, pl.ds(width + row, 1), :]
            alpha_two = full32[0, block]
            beta_two = full32[1, block]
            where = pl.ds(row * LB, LB)
            pair[where, :R] = (alpha_one * beta_two + beta_one * alpha_two).astype(BF16)
            pair[where, R:] = (beta_one * beta_two).astype(BF16)
        values = jnp.dot(pair[...], slab_t[...], preferred_element_type=F32)
        l_second = 2 + two * LB + lax.broadcasted_iota(jnp.int32, (LB, LB), 0)
        l_third = 2 + (NB - 1) * LB + lax.broadcasted_iota(jnp.int32, (LB, LB), 1)
        for row in range(width):
            l_first = 2 + one * LB + row_offset + row
            keep = (
                ((l_first + l_second + l_third) % 2 == 0)
                & (l_first <= l_second)
                & (l_second <= l_third)
                & (l_third <= l_first + l_second)
            )
            out_ref[0, row] = jnp.where(keep, values[row * LB : (row + 1) * LB], 0.0).astype(BF16)

    @pl.when(jnp.logical_not(live))
    def _():
        out_ref[...] = jnp.zeros(out_ref.shape, BF16)


def tiles(place, tile_list, first, own, other, scale):
    slots = tile_list.shape[0]
    width = own.shape[2]
    whole = lambda a: pl.BlockSpec(a.shape, lambda i: (0,) * a.ndim)
    return pl.pallas_call(
        tile_kernel,
        grid=(slots,),
        in_specs=[
            pl.BlockSpec(memory_space=pltpu.SMEM),
            pl.BlockSpec(memory_space=pltpu.SMEM),
            whole(first),
            whole(own),
            whole(other),
            whole(scale),
        ],
        out_specs=pl.BlockSpec((1, width, LB, LB), lambda i: (i, 0, 0, 0)),
        out_shape=jax.ShapeDtypeStruct((slots, width, LB, LB), BF16),
        scratch_shapes=[
            pltpu.VMEM(first.shape, F32),
            pltpu.VMEM((2, FULL, LB, R), F32),
            pltpu.VMEM((2 * R, LB), BF16),
            pltpu.VMEM((width * LB, 2 * R), BF16),
        ],
        compiler_params=pltpu.CompilerParams(vmem_limit_bytes=48 << 20),
        name="tiles",
    )(place, tile_list, first, own, other, scale)


def body(transfer, bessel_table, k_weight, power_spectrum, radial_weight, tile_list):
    band_count = lax.axis_size("band")
    ka_count = lax.axis_size("ka")
    width = LB // ka_count
    depth = transfer.shape[1]
    band = lax.axis_index("band")
    core = band % 2

    scaled = transfer.astype(F32) * k_weight[None, :]
    weighted = jnp.stack([scaled, scaled * power_spectrum[None, :]], axis=0).astype(BF16)
    weighted = weighted.reshape(2, ka_count, width, 1, depth).transpose(1, 0, 2, 3, 4)
    same = jnp.eye(width, dtype=jnp.bool_)[None, None, :, :, None]
    weights = jnp.where(same, weighted, jnp.zeros((), BF16)).reshape(ka_count, 2 * width, width * depth)

    partial = project(weights, bessel_table, 8)
    shares = lax.all_to_all(partial, "ka", 0, 0, tiled=True)
    rows = jnp.sum(shares.astype(F32), axis=0).astype(BF16)
    copies = jnp.broadcast_to(rows[None], (band_count,) + rows.shape)
    first = lax.all_to_all(copies, "band", 0, 0, tiled=True)

    mine = lax.dynamic_slice_in_dim(first.reshape(NB, 2, width, R)[LOW:], core, 1, 1)[:, 0]
    mine = jnp.broadcast_to(mine[None], (ka_count,) + mine.shape)
    own = lax.all_to_all(mine, "ka", 0, 0, tiled=True)
    other = lax.ppermute(own, "band", [(i, i ^ 1) for i in range(band_count)])

    scale = (radial_weight * (0.5 / math.sqrt(R)))[None, :]
    place = jnp.stack([core, lax.axis_index("ka") * width]).astype(jnp.int32)
    return tiles(place, tile_list, first, own, other, scale)


def solution(mesh):
    return jax.shard_map(
        body,
        mesh=mesh,
        in_specs=(P("band", "ka"), P("band", "ka", None), P("ka"), P("ka"), P(), P("band", None)),
        out_specs=P("band", "ka", None, None),
        check_vma=False,
    )
```

```python
import math

import jax
import jax.numpy as jnp
from jax import lax
from jax.experimental import pallas as pl
from jax.experimental.pallas import tpu as pltpu
from jax.sharding import PartitionSpec as P

NB = 8
LB = 128
R = 640
LOW = 3
FULL = NB - LOW
NX = 4
F32 = jnp.float32
BF16 = jnp.bfloat16

VMEM = pl.BlockSpec(memory_space=pltpu.VMEM)
SMEM = pl.BlockSpec(memory_space=pltpu.SMEM)
HBM = pl.BlockSpec(memory_space=pltpu.HBM)


def project_kernel(transfer_ref, weight_ref, power_ref, bessel_ref, out_ref, table, weights, sems):
    chunks = sems.shape[0]
    rows = table.shape[0] // chunks
    depth = table.shape[1]
    dests = out_ref.shape[0]
    width = LB // dests

    def fetch(i):
        part = pl.ds(i * rows, rows)
        return pltpu.make_async_copy(bessel_ref.at[part], table.at[part], sems.at[i])

    for i in range(chunks):
        fetch(i).start()
    alpha = transfer_ref[...].astype(F32).T * weight_ref[...]
    beta = alpha * power_ref[...]
    wide = (LB, width * depth)
    same = lax.broadcasted_iota(jnp.int32, wide, 0) % width == lax.broadcasted_iota(jnp.int32, wide, 1) // depth
    alpha = jnp.where(same, jnp.concatenate([alpha] * width, axis=1), 0.0)
    beta = jnp.where(same, jnp.concatenate([beta] * width, axis=1), 0.0)
    for dest in range(dests):
        weights[dest, :width] = alpha[dest * width : (dest + 1) * width]
        weights[dest, width:] = beta[dest * width : (dest + 1) * width]
    for i in range(chunks):
        fetch(i).wait()
        for dest in range(i * dests // chunks, (i + 1) * dests // chunks):
            part = table[dest * width : (dest + 1) * width].reshape(width * depth, R)
            out_ref[dest] = jnp.dot(weights[dest].astype(BF16), part, preferred_element_type=F32).astype(BF16)


def project(transfer, k_weight, power_spectrum, bessel, dests, chunks=8):
    width = LB // dests
    depth = transfer.shape[1]
    return pl.pallas_call(
        project_kernel,
        in_specs=[VMEM, VMEM, VMEM, HBM],
        out_specs=VMEM,
        out_shape=jax.ShapeDtypeStruct((dests, 2 * width, R), BF16),
        scratch_shapes=[
            pltpu.VMEM(bessel.shape, BF16),
            pltpu.VMEM((dests, 2 * width, width * depth), F32),
            pltpu.SemaphoreType.DMA((chunks,)),
        ],
        compiler_params=pltpu.CompilerParams(vmem_limit_bytes=58 << 20),
        name="project",
    )(transfer.T, k_weight[None, :], power_spectrum[None, :], bessel)


def total_kernel(shares_ref, out_ref):
    total = shares_ref[0].astype(F32)
    for part in range(1, shares_ref.shape[0]):
        total = total + shares_ref[part].astype(F32)
    total = total.astype(BF16)
    for copy in range(out_ref.shape[0]):
        out_ref[copy] = total


def half_kernel(first_ref, out_ref, stage):
    core = lax.axis_index("band") % 2
    width = first_ref.shape[1] // 2
    for block in range(FULL):
        rows = first_ref[LOW + block].astype(F32)
        stage[block * width : (block + 1) * width] = jnp.where(core == 0, rows[:width], rows[width:])
    rows = stage[...].astype(BF16)
    for copy in range(out_ref.shape[0]):
        out_ref[copy] = rows


def line_kernel(line_ref, out_ref, stage):
    parts = line_ref.shape[0]
    width = line_ref.shape[1] // FULL
    for part in range(parts):
        rows = line_ref[part].astype(F32)
        for block in range(FULL):
            start = (block * parts + part) * width
            stage[start : start + width] = rows[block * width : (block + 1) * width]
    rows = stage[...].astype(BF16)
    for copy in range(out_ref.shape[0]):
        out_ref[copy] = rows


def spread(kernel, source, copies, rows, staged=True):
    return pl.pallas_call(
        kernel,
        in_specs=[VMEM],
        out_specs=VMEM,
        out_shape=jax.ShapeDtypeStruct((copies, rows, R), BF16),
        scratch_shapes=[pltpu.VMEM((rows, R), F32)] if staged else [],
        compiler_params=pltpu.CompilerParams(vmem_limit_bytes=16 << 20),
        name=kernel.__name__,
    )(source)


def place_rows(source, block, stripe, width):
    columns = source.shape[0]
    rows = [source[column, block * stripe : (block + 1) * stripe].astype(F32) for column in range(columns)]
    pieces = [rows[column][part * width : (part + 1) * width] for part in range(stripe // width) for column in range(columns)]
    return jnp.concatenate(pieces, axis=0)


def tile_kernel(tiles_ref, first_ref, own_ref, other_ref, scale_ref, out_ref, first32, full, slab_t, pair, held, sems):
    core = lax.axis_index("band") % 2
    stripe = own_ref.shape[1] // FULL
    width = first_ref.shape[1] // 2
    row_offset = lax.axis_index("ka") * width
    slots = held.shape[0]

    def send(slot):
        return pltpu.make_async_copy(held.at[slot], out_ref.at[slot], sems.at[slot])

    first32[...] = first_ref[...].astype(F32)
    scale = scale_ref[...] * (0.5 / math.sqrt(R))
    for kind, source in ((core, own_ref), (1 - core, other_ref)):
        for block in range(FULL):
            rows = place_rows(source, block, stripe, width)
            full[kind, block] = rows.astype(BF16)
            if block == FULL - 1:
                slab_t[1 - kind] = (rows * scale).T.astype(BF16)

    def one_slot(slot, carry):
        one = tiles_ref[0, slot]
        two = tiles_ref[1, slot]
        live = (one >= 0) & (one + two >= NB - LOW)

        @pl.when(live)
        def _():
            block = two - LOW
            for row in range(width):
                alpha_one = jnp.broadcast_to(first32[one, pl.ds(row, 1), :], (LB, R)).astype(BF16)
                beta_one = jnp.broadcast_to(first32[one, pl.ds(width + row, 1), :], (LB, R)).astype(BF16)
                alpha_two = full[0, block]
                beta_two = full[1, block]
                where = pl.ds(row * LB, LB)
                pair[where, :R] = alpha_one * beta_two + beta_one * alpha_two
                pair[where, R:] = beta_one * beta_two
            values = jnp.dot(pair[...], slab_t[...].reshape(2 * R, LB), preferred_element_type=F32)
            second = lax.broadcasted_iota(jnp.int32, (LB, LB), 0) + two * LB
            third = lax.broadcasted_iota(jnp.int32, (LB, LB), 1) + (NB - 1) * LB
            gap = third - second - 2
            floor = [jnp.where((second <= third) & (gap % 2 == odd), gap, NB * LB) for odd in (0, 1)]
            for row in range(width):
                first = one * LB + row_offset + row
                keep = (first >= floor[row % 2]) & (first <= second)
                held[slot, row] = jnp.where(keep, values[row * LB : (row + 1) * LB], 0.0).astype(BF16)

        @pl.when(jnp.logical_not(live))
        def _():
            held[slot] = jnp.zeros(held.shape[1:], BF16)

        send(slot).start()
        return carry

    lax.fori_loop(0, slots, one_slot, 0)
    for slot in range(slots):
        send(slot).wait()


def tiles(tile_list, first, own, other, scale):
    slots = tile_list.shape[0]
    width = first.shape[1] // 2
    shape = (slots, width, LB, LB)
    return pl.pallas_call(
        tile_kernel,
        in_specs=[SMEM, VMEM, VMEM, VMEM, VMEM],
        out_specs=HBM,
        out_shape=jax.ShapeDtypeStruct(shape, BF16),
        scratch_shapes=[
            pltpu.VMEM(first.shape, F32),
            pltpu.VMEM((2, FULL, LB, R), BF16),
            pltpu.VMEM((2, R, LB), BF16),
            pltpu.VMEM((width * LB, 2 * R), BF16),
            pltpu.VMEM(shape, BF16),
            pltpu.SemaphoreType.DMA((slots,)),
        ],
        compiler_params=pltpu.CompilerParams(vmem_limit_bytes=40 << 20),
        name="tiles",
    )(tile_list.T, first, own, other, scale)


def body(transfer, bessel_table, k_weight, power_spectrum, radial_weight, tile_list):
    bands = lax.axis_size("band")
    members = lax.axis_size("ka")
    width = LB // members
    depth = members // NX
    along_x = [[z * NX + x for x in range(NX)] for z in range(depth)]
    along_z = [[z * NX + x for z in range(depth)] for x in range(NX)]

    partial = project(transfer, k_weight, power_spectrum, bessel_table, members)
    shares = lax.all_to_all(partial, "ka", 0, 0, tiled=True)
    copies = spread(total_kernel, shares, bands, 2 * width, staged=False)
    first = lax.all_to_all(copies, "band", 0, 0, tiled=True)

    copies = spread(half_kernel, first, depth, FULL * width)
    line = lax.all_to_all(copies, "ka", 0, 0, axis_index_groups=along_z, tiled=True)
    copies = spread(line_kernel, line, NX, FULL * width * depth)
    own = lax.all_to_all(copies, "ka", 0, 0, axis_index_groups=along_x, tiled=True)
    other = lax.ppermute(own, "band", [(i, i ^ 1) for i in range(bands)])

    return tiles(tile_list, first, own, other, radial_weight[None, :])


def solution(mesh):
    return jax.shard_map(
        body,
        mesh=mesh,
        in_specs=(P("band", "ka"), P("band", "ka", None), P("ka"), P("ka"), P(), P("band", None)),
        out_specs=P("band", "ka", None, None),
        check_vma=False,
    )
```

```python
import math

import jax
import jax.numpy as jnp
from jax import lax
from jax.experimental import pallas as pl
from jax.experimental.pallas import tpu as pltpu
from jax.sharding import PartitionSpec as P

NB = 8
LB = 128
R = 640
LOW = 3
FULL = NB - LOW
NX = 4
F32 = jnp.float32
BF16 = jnp.bfloat16

VMEM = pl.BlockSpec(memory_space=pltpu.VMEM)
SMEM = pl.BlockSpec(memory_space=pltpu.SMEM)
HBM = pl.BlockSpec(memory_space=pltpu.HBM)


def project_kernel(transfer_ref, weight_ref, power_ref, bessel_ref, out_ref, table, weights, sems):
    chunks = sems.shape[0]
    rows = table.shape[0] // chunks
    depth = table.shape[1]
    dests = out_ref.shape[0]
    width = LB // dests

    def fetch(i):
        part = pl.ds(i * rows, rows)
        return pltpu.make_async_copy(bessel_ref.at[part], table.at[part], sems.at[i])

    for i in range(chunks):
        fetch(i).start()
    alpha = transfer_ref[...].astype(F32).T * weight_ref[...]
    beta = alpha * power_ref[...]
    wide = (LB, width * depth)
    same = lax.broadcasted_iota(jnp.int32, wide, 0) % width == lax.broadcasted_iota(jnp.int32, wide, 1) // depth
    alpha = jnp.where(same, jnp.concatenate([alpha] * width, axis=1), 0.0)
    beta = jnp.where(same, jnp.concatenate([beta] * width, axis=1), 0.0)
    for dest in range(dests):
        weights[dest, :width] = alpha[dest * width : (dest + 1) * width]
        weights[dest, width:] = beta[dest * width : (dest + 1) * width]
    for i in range(chunks):
        fetch(i).wait()
        for dest in range(i * dests // chunks, (i + 1) * dests // chunks):
            part = table[dest * width : (dest + 1) * width].reshape(width * depth, R)
            out_ref[dest] = jnp.dot(weights[dest].astype(BF16), part, preferred_element_type=F32).astype(BF16)


def project(transfer, k_weight, power_spectrum, bessel, dests, chunks=8):
    width = LB // dests
    depth = transfer.shape[1]
    return pl.pallas_call(
        project_kernel,
        in_specs=[VMEM, VMEM, VMEM, HBM],
        out_specs=VMEM,
        out_shape=jax.ShapeDtypeStruct((dests, 2 * width, R), BF16),
        scratch_shapes=[
            pltpu.VMEM(bessel.shape, BF16),
            pltpu.VMEM((dests, 2 * width, width * depth), F32),
            pltpu.SemaphoreType.DMA((chunks,)),
        ],
        compiler_params=pltpu.CompilerParams(vmem_limit_bytes=58 << 20),
        name="project",
    )(transfer.T, k_weight[None, :], power_spectrum[None, :], bessel)


def total_kernel(shares_ref, keep_ref, give_ref):
    core = lax.axis_index("band") % 2
    total = shares_ref[0].astype(F32)
    for part in range(1, shares_ref.shape[0]):
        total = total + shares_ref[part].astype(F32)
    width = total.shape[0] // 2
    alpha, beta = total[:width], total[width:]
    keep_ref[...] = jnp.where(core == 0, alpha, beta).astype(BF16)
    give_ref[...] = jnp.where(core == 0, beta, alpha).astype(BF16)


def total(shares):
    half = jax.ShapeDtypeStruct((shares.shape[1] // 2, R), BF16)
    return pl.pallas_call(
        total_kernel,
        in_specs=[VMEM],
        out_specs=[VMEM, VMEM],
        out_shape=[half, half],
        compiler_params=pltpu.CompilerParams(vmem_limit_bytes=16 << 20),
        name="total",
    )(shares)


def couple_kernel(keep_ref, got_ref, out_ref):
    core = lax.axis_index("band") % 2
    keep = keep_ref[...].astype(F32)
    got = got_ref[...].astype(F32)
    low = jnp.where(core == 0, keep, got)
    high = jnp.where(core == 0, got, keep)
    rows = jnp.concatenate([low, high], axis=0).astype(BF16)
    for copy in range(out_ref.shape[0]):
        out_ref[copy] = rows


def couple(keep, got, copies):
    return pl.pallas_call(
        couple_kernel,
        in_specs=[VMEM, VMEM],
        out_specs=VMEM,
        out_shape=jax.ShapeDtypeStruct((copies, 2 * keep.shape[0], R), BF16),
        compiler_params=pltpu.CompilerParams(vmem_limit_bytes=16 << 20),
        name="couple",
    )(keep, got)


def line_kernel(line_ref, out_ref, mine_ref):
    parts = line_ref.shape[0] // (NB // 2)
    width = line_ref.shape[1] // 2
    here = lax.axis_index("ka") // NX
    for pair in range(NB // 2):
        mine_ref[pair] = line_ref[pair * parts + here]
    pieces = []
    for block in range(LOW, NB):
        for part in range(parts):
            rows = line_ref[block // 2 * parts + part].astype(F32)
            start = block % 2 * width
            pieces.append(rows[start : start + width])
    rows = jnp.concatenate(pieces, axis=0).astype(BF16)
    for copy in range(out_ref.shape[0]):
        out_ref[copy] = rows


def spread_line(line):
    members, rows, _ = line.shape
    parts = members // (NB // 2)
    return pl.pallas_call(
        line_kernel,
        in_specs=[VMEM],
        out_specs=[VMEM, VMEM],
        out_shape=[
            jax.ShapeDtypeStruct((NX, FULL * parts * rows // 2, R), BF16),
            jax.ShapeDtypeStruct((NB // 2, rows, R), BF16),
        ],
        compiler_params=pltpu.CompilerParams(vmem_limit_bytes=16 << 20),
        name="spread_line",
    )(line)


def place_rows(source, block, stripe, width):
    columns = source.shape[0]
    rows = [source[column, block * stripe : (block + 1) * stripe].astype(F32) for column in range(columns)]
    pieces = [rows[column][part * width : (part + 1) * width] for part in range(stripe // width) for column in range(columns)]
    return jnp.concatenate(pieces, axis=0)


def tile_kernel(tiles_ref, mine_ref, theirs_ref, own_ref, other_ref, scale_ref, out_ref, first32, full, slab_t, pair, held, sems):
    core = lax.axis_index("band") % 2
    stripe = own_ref.shape[1] // FULL
    width = mine_ref.shape[1] // 2
    row_offset = lax.axis_index("ka") * width
    slots = held.shape[0]

    def send(slot):
        return pltpu.make_async_copy(held.at[slot], out_ref.at[slot], sems.at[slot])

    for kind, source in ((core, mine_ref), (1 - core, theirs_ref)):
        for block in range(NB):
            start = block % 2 * width
            first32[kind, block] = source[block // 2].astype(F32)[start : start + width]
    scale = scale_ref[...] * (0.5 / math.sqrt(R))
    for kind, source in ((core, own_ref), (1 - core, other_ref)):
        for block in range(FULL):
            rows = place_rows(source, block, stripe, width)
            full[kind, block] = rows.astype(BF16)
            if block == FULL - 1:
                slab_t[1 - kind] = (rows * scale).T.astype(BF16)

    def one_slot(slot, carry):
        one = tiles_ref[0, slot]
        two = tiles_ref[1, slot]
        live = (one >= 0) & (one + two >= NB - LOW)

        @pl.when(live)
        def _():
            block = two - LOW
            for row in range(width):
                alpha_one = jnp.broadcast_to(first32[0, one, pl.ds(row, 1), :], (LB, R)).astype(BF16)
                beta_one = jnp.broadcast_to(first32[1, one, pl.ds(row, 1), :], (LB, R)).astype(BF16)
                alpha_two = full[0, block]
                beta_two = full[1, block]
                where = pl.ds(row * LB, LB)
                pair[where, :R] = alpha_one * beta_two + beta_one * alpha_two
                pair[where, R:] = beta_one * beta_two
            values = jnp.dot(pair[...], slab_t[...].reshape(2 * R, LB), preferred_element_type=F32)
            second = lax.broadcasted_iota(jnp.int32, (LB, LB), 0) + two * LB
            third = lax.broadcasted_iota(jnp.int32, (LB, LB), 1) + (NB - 1) * LB
            gap = third - second - 2
            floor = [jnp.where((second <= third) & (gap % 2 == odd), gap, NB * LB) for odd in (0, 1)]
            for row in range(width):
                first = one * LB + row_offset + row
                keep = (first >= floor[row % 2]) & (first <= second)
                held[slot, row] = jnp.where(keep, values[row * LB : (row + 1) * LB], 0.0).astype(BF16)

        @pl.when(jnp.logical_not(live))
        def _():
            held[slot] = jnp.zeros(held.shape[1:], BF16)

        send(slot).start()
        return carry

    lax.fori_loop(0, slots, one_slot, 0)
    for slot in range(slots):
        send(slot).wait()


def tiles(tile_list, mine, theirs, own, other, scale):
    slots = tile_list.shape[0]
    width = mine.shape[1] // 2
    shape = (slots, width, LB, LB)
    return pl.pallas_call(
        tile_kernel,
        in_specs=[SMEM, VMEM, VMEM, VMEM, VMEM, VMEM],
        out_specs=HBM,
        out_shape=jax.ShapeDtypeStruct(shape, BF16),
        scratch_shapes=[
            pltpu.VMEM((2, NB, width, R), F32),
            pltpu.VMEM((2, FULL, LB, R), BF16),
            pltpu.VMEM((2, R, LB), BF16),
            pltpu.VMEM((width * LB, 2 * R), BF16),
            pltpu.VMEM(shape, BF16),
            pltpu.SemaphoreType.DMA((slots,)),
        ],
        compiler_params=pltpu.CompilerParams(vmem_limit_bytes=40 << 20),
        name="tiles",
    )(tile_list.T, mine, theirs, own, other, scale)


def body(transfer, bessel_table, k_weight, power_spectrum, radial_weight, tile_list):
    bands = lax.axis_size("band")
    members = lax.axis_size("ka")
    depth = members // NX
    along_x = [[z * NX + x for x in range(NX)] for z in range(depth)]
    along_yz = [
        [(y * 2 + core) * members + z * NX + x for y in range(bands // 2) for z in range(depth)]
        for core in range(2)
        for x in range(NX)
    ]
    sibling = [(i, i ^ 1) for i in range(bands)]

    partial = project(transfer, k_weight, power_spectrum, bessel_table, members)
    shares = lax.all_to_all(partial, "ka", 0, 0, tiled=True)
    keep, give = total(shares)
    got = lax.ppermute(give, "band", sibling)
    copies = couple(keep, got, len(along_yz[0]))
    line = lax.all_to_all(copies, ("band", "ka"), 0, 0, axis_index_groups=along_yz, tiled=True)
    copies, mine = spread_line(line)
    theirs = lax.ppermute(mine, "band", sibling)
    own = lax.all_to_all(copies, "ka", 0, 0, axis_index_groups=along_x, tiled=True)
    other = lax.ppermute(own, "band", sibling)
    return tiles(tile_list, mine, theirs, own, other, radial_weight[None, :])


def solution(mesh):
    return jax.shard_map(
        body,
        mesh=mesh,
        in_specs=(P("band", "ka"), P("band", "ka", None), P("ka"), P("ka"), P(), P("band", None)),
        out_specs=P("band", "ka", None, None),
        check_vma=False,
    )
```

```python
import math

import jax
import jax.numpy as jnp
from jax import lax
from jax.experimental import pallas as pl
from jax.experimental.pallas import tpu as pltpu
from jax.sharding import PartitionSpec as P

NB = 8
LB = 128
R = 640
LOW = 3
FULL = NB - LOW
PAIRS = ((2, 0), (3, 0), (1, 3))
NX = 4
F32 = jnp.float32
BF16 = jnp.bfloat16

VMEM = pl.BlockSpec(memory_space=pltpu.VMEM)
SMEM = pl.BlockSpec(memory_space=pltpu.SMEM)
HBM = pl.BlockSpec(memory_space=pltpu.HBM)


def project_kernel(transfer_ref, weight_ref, power_ref, bessel_ref, out_ref, table, weights, sems):
    chunks = sems.shape[0]
    rows = table.shape[0] // chunks
    depth = table.shape[1]
    dests = out_ref.shape[0]
    width = LB // dests

    def fetch(i):
        part = pl.ds(i * rows, rows)
        return pltpu.make_async_copy(bessel_ref.at[part], table.at[part], sems.at[i])

    for i in range(chunks):
        fetch(i).start()
    alpha = transfer_ref[...].astype(F32).T * weight_ref[...]
    beta = alpha * power_ref[...]
    wide = (LB, width * depth)
    same = lax.broadcasted_iota(jnp.int32, wide, 0) % width == lax.broadcasted_iota(jnp.int32, wide, 1) // depth
    alpha = jnp.where(same, jnp.concatenate([alpha] * width, axis=1), 0.0)
    beta = jnp.where(same, jnp.concatenate([beta] * width, axis=1), 0.0)
    for dest in range(dests):
        weights[dest, :width] = alpha[dest * width : (dest + 1) * width]
        weights[dest, width:] = beta[dest * width : (dest + 1) * width]
    for i in range(chunks):
        fetch(i).wait()
        for dest in range(i * dests // chunks, (i + 1) * dests // chunks):
            part = table[dest * width : (dest + 1) * width].reshape(width * depth, R)
            out_ref[dest] = jnp.dot(weights[dest].astype(BF16), part, preferred_element_type=F32).astype(BF16)


def project(transfer, k_weight, power_spectrum, bessel, dests, chunks=8):
    width = LB // dests
    depth = transfer.shape[1]
    return pl.pallas_call(
        project_kernel,
        in_specs=[VMEM, VMEM, VMEM, HBM],
        out_specs=VMEM,
        out_shape=jax.ShapeDtypeStruct((dests, 2 * width, R), BF16),
        scratch_shapes=[
            pltpu.VMEM(bessel.shape, BF16),
            pltpu.VMEM((dests, 2 * width, width * depth), F32),
            pltpu.SemaphoreType.DMA((chunks,)),
        ],
        compiler_params=pltpu.CompilerParams(vmem_limit_bytes=58 << 20),
        name="project",
    )(transfer.T, k_weight[None, :], power_spectrum[None, :], bessel)


def total_kernel(shares_ref, out_ref):
    total = shares_ref[0].astype(F32)
    for part in range(1, shares_ref.shape[0]):
        total = total + shares_ref[part].astype(F32)
    total = total.astype(BF16)
    for copy in range(out_ref.shape[0]):
        out_ref[copy] = total


def total(shares, copies):
    return pl.pallas_call(
        total_kernel,
        in_specs=[VMEM],
        out_specs=VMEM,
        out_shape=jax.ShapeDtypeStruct((copies,) + shares.shape[1:], BF16),
        compiler_params=pltpu.CompilerParams(vmem_limit_bytes=16 << 20),
        name="total",
    )(shares)


def line_kernel(line_ref, out_ref, mine_ref, stage):
    pairs = NB // 2
    parts = line_ref.shape[0] // pairs
    rows = line_ref.shape[1]
    here = lax.axis_index("ka") // NX
    for pair in range(pairs):
        mine_ref[pair] = line_ref[pair * parts + here]
    start = 0
    for pair, skip in PAIRS:
        for part in range(skip, parts):
            stage[start : start + rows] = line_ref[pair * parts + part].astype(F32)
            start += rows
    values = stage[...].astype(BF16)
    for copy in range(out_ref.shape[0]):
        out_ref[copy] = values


def spread_line(line):
    members, rows, _ = line.shape
    parts = members // (NB // 2)
    height = sum(parts - skip for _, skip in PAIRS) * rows
    return pl.pallas_call(
        line_kernel,
        in_specs=[VMEM],
        out_specs=[VMEM, VMEM],
        out_shape=[
            jax.ShapeDtypeStruct((NX, height, R), BF16),
            jax.ShapeDtypeStruct((NB // 2, rows, R), BF16),
        ],
        scratch_shapes=[pltpu.VMEM((height, R), F32)],
        compiler_params=pltpu.CompilerParams(vmem_limit_bytes=16 << 20),
        name="spread_line",
    )(line)


def place_rows(source, full, parity, width):
    columns = source.shape[0]
    parts = LB // (columns * width)
    values = [source[column].astype(F32) for column in range(columns)]
    start = 0
    for pair, skip in PAIRS:
        for kind in range(2):
            pieces = []
            for part in range(skip, parts):
                row = start + ((part - skip) * 2 + kind) * width
                pieces += [values[column][row : row + width] for column in range(columns)]
            rows = jnp.concatenate(pieces, axis=0).astype(BF16)
            if skip == 0:
                full[kind, 2 * pair + parity - LOW] = rows
            else:
                @pl.when(parity == 1)
                def _():
                    full[kind, 0, skip * columns * width :] = rows
                    full[kind, 0, : skip * columns * width] = jnp.zeros((skip * columns * width, R), BF16)
        start += (parts - skip) * 2 * width


def tile_kernel(tiles_ref, mine_ref, theirs_ref, own_ref, other_ref, scale_ref, out_ref, first32, full, slab_t, pair, held, sems):
    core = lax.axis_index("band") % 2
    width = mine_ref.shape[1] // 2
    row_offset = lax.axis_index("ka") * width
    slots = held.shape[0]

    def send(slot):
        return pltpu.make_async_copy(held.at[slot], out_ref.at[slot], sems.at[slot])

    for parity, source in ((core, mine_ref), (1 - core, theirs_ref)):
        for couple in range(NB // 2):
            first32[2 * couple + parity] = source[couple].astype(F32)
    place_rows(own_ref, full, core, width)
    place_rows(other_ref, full, 1 - core, width)
    scale = scale_ref[...] * (0.5 / math.sqrt(R))
    for kind in range(2):
        slab_t[1 - kind] = (full[kind, FULL - 1].astype(F32) * scale).T.astype(BF16)

    def one_slot(slot, carry):
        one = tiles_ref[0, slot]
        two = tiles_ref[1, slot]
        live = (one >= 0) & (one + two >= NB - LOW)

        @pl.when(live)
        def _():
            block = two - LOW
            for row in range(width):
                alpha_one = jnp.broadcast_to(first32[one, pl.ds(row, 1), :], (LB, R)).astype(BF16)
                beta_one = jnp.broadcast_to(first32[one, pl.ds(width + row, 1), :], (LB, R)).astype(BF16)
                alpha_two = full[0, block]
                beta_two = full[1, block]
                where = pl.ds(row * LB, LB)
                pair[where, :R] = alpha_one * beta_two + beta_one * alpha_two
                pair[where, R:] = beta_one * beta_two
            values = jnp.dot(pair[...], slab_t[...].reshape(2 * R, LB), preferred_element_type=F32)
            second = lax.broadcasted_iota(jnp.int32, (LB, LB), 0) + two * LB
            third = lax.broadcasted_iota(jnp.int32, (LB, LB), 1) + (NB - 1) * LB
            gap = third - second - 2
            floor = [jnp.where((second <= third) & (gap % 2 == odd), gap, NB * LB) for odd in (0, 1)]
            for row in range(width):
                first = one * LB + row_offset + row
                keep = (first >= floor[row % 2]) & (first <= second)
                held[slot, row] = jnp.where(keep, values[row * LB : (row + 1) * LB], 0.0).astype(BF16)

        @pl.when(jnp.logical_not(live))
        def _():
            held[slot] = jnp.zeros(held.shape[1:], BF16)

        send(slot).start()
        return carry

    lax.fori_loop(0, slots, one_slot, 0)
    for slot in range(slots):
        send(slot).wait()


def tiles(tile_list, mine, theirs, own, other, scale):
    slots = tile_list.shape[0]
    width = mine.shape[1] // 2
    shape = (slots, width, LB, LB)
    return pl.pallas_call(
        tile_kernel,
        in_specs=[SMEM, VMEM, VMEM, VMEM, VMEM, VMEM],
        out_specs=HBM,
        out_shape=jax.ShapeDtypeStruct(shape, BF16),
        scratch_shapes=[
            pltpu.VMEM((NB, 2 * width, R), F32),
            pltpu.VMEM((2, FULL, LB, R), BF16),
            pltpu.VMEM((2, R, LB), BF16),
            pltpu.VMEM((width * LB, 2 * R), BF16),
            pltpu.VMEM(shape, BF16),
            pltpu.SemaphoreType.DMA((slots,)),
        ],
        compiler_params=pltpu.CompilerParams(vmem_limit_bytes=40 << 20),
        name="tiles",
    )(tile_list.T, mine, theirs, own, other, scale)


def body(transfer, bessel_table, k_weight, power_spectrum, radial_weight, tile_list):
    bands = lax.axis_size("band")
    members = lax.axis_size("ka")
    depth = members // NX
    along_x = [[z * NX + x for x in range(NX)] for z in range(depth)]
    along_yz = [
        [(y * 2 + core) * members + z * NX + x for y in range(bands // 2) for z in range(depth)]
        for core in range(2)
        for x in range(NX)
    ]
    sibling = [(i, i ^ 1) for i in range(bands)]

    partial = project(transfer, k_weight, power_spectrum, bessel_table, members)
    shares = lax.all_to_all(partial, "ka", 0, 0, tiled=True)
    copies = total(shares, len(along_yz[0]))
    line = lax.all_to_all(copies, ("band", "ka"), 0, 0, axis_index_groups=along_yz, tiled=True)
    copies, mine = spread_line(line)
    theirs = lax.ppermute(mine, "band", sibling)
    own = lax.all_to_all(copies, "ka", 0, 0, axis_index_groups=along_x, tiled=True)
    other = lax.ppermute(own, "band", sibling)
    return tiles(tile_list, mine, theirs, own, other, radial_weight[None, :])


def solution(mesh):
    return jax.shard_map(
        body,
        mesh=mesh,
        in_specs=(P("band", "ka"), P("band", "ka", None), P("ka"), P("ka"), P(), P("band", None)),
        out_specs=P("band", "ka", None, None),
        check_vma=False,
    )
```

```python
import math

import jax
import jax.numpy as jnp
from jax import lax
from jax.experimental import pallas as pl
from jax.experimental.pallas import tpu as pltpu
from jax.sharding import PartitionSpec as P

NB = 8
LB = 128
R = 640
LOW = 3
FULL = NB - LOW
PAIRS = ((2, 0), (3, 0), (1, 3))
NX = 4
F32 = jnp.float32
BF16 = jnp.bfloat16

VMEM = pl.BlockSpec(memory_space=pltpu.VMEM)
SMEM = pl.BlockSpec(memory_space=pltpu.SMEM)
HBM = pl.BlockSpec(memory_space=pltpu.HBM)


def project_kernel(transfer_ref, weight_ref, power_ref, bessel_ref, out_ref, table, weights, sems):
    chunks = sems.shape[0]
    rows = table.shape[0] // chunks
    depth = table.shape[1]
    dests = out_ref.shape[0]
    width = LB // dests

    def fetch(i):
        part = pl.ds(i * rows, rows)
        return pltpu.make_async_copy(bessel_ref.at[part], table.at[part], sems.at[i])

    for i in range(chunks):
        fetch(i).start()
    alpha = transfer_ref[...].astype(F32).T * weight_ref[...]
    beta = alpha * power_ref[...]
    wide = (LB, width * depth)
    same = lax.broadcasted_iota(jnp.int32, wide, 0) % width == lax.broadcasted_iota(jnp.int32, wide, 1) // depth
    alpha = jnp.where(same, jnp.concatenate([alpha] * width, axis=1), 0.0)
    beta = jnp.where(same, jnp.concatenate([beta] * width, axis=1), 0.0)
    for dest in range(dests):
        weights[dest, :width] = alpha[dest * width : (dest + 1) * width]
        weights[dest, width:] = beta[dest * width : (dest + 1) * width]
    for i in range(chunks):
        fetch(i).wait()
        for dest in range(i * dests // chunks, (i + 1) * dests // chunks):
            part = table[dest * width : (dest + 1) * width].reshape(width * depth, R)
            out_ref[dest] = jnp.dot(weights[dest].astype(BF16), part, preferred_element_type=F32).astype(BF16)


def project(transfer, k_weight, power_spectrum, bessel, dests, chunks=8):
    width = LB // dests
    depth = transfer.shape[1]
    return pl.pallas_call(
        project_kernel,
        in_specs=[VMEM, VMEM, VMEM, HBM],
        out_specs=VMEM,
        out_shape=jax.ShapeDtypeStruct((dests, 2 * width, R), BF16),
        scratch_shapes=[
            pltpu.VMEM(bessel.shape, BF16),
            pltpu.VMEM((dests, 2 * width, width * depth), F32),
            pltpu.SemaphoreType.DMA((chunks,)),
        ],
        compiler_params=pltpu.CompilerParams(vmem_limit_bytes=58 << 20),
        name="project",
    )(transfer.T, k_weight[None, :], power_spectrum[None, :], bessel)


def total_kernel(shares_ref, out_ref):
    total = shares_ref[0].astype(F32)
    for part in range(1, shares_ref.shape[0]):
        total = total + shares_ref[part].astype(F32)
    total = total.astype(BF16)
    for copy in range(out_ref.shape[0]):
        out_ref[copy] = total


def total(shares, copies):
    return pl.pallas_call(
        total_kernel,
        in_specs=[VMEM],
        out_specs=VMEM,
        out_shape=jax.ShapeDtypeStruct((copies,) + shares.shape[1:], BF16),
        compiler_params=pltpu.CompilerParams(vmem_limit_bytes=16 << 20),
        name="total",
    )(shares)


def line_kernel(line_ref, out_ref, mine_ref, stage):
    pairs = NB // 2
    parts = line_ref.shape[0] // pairs
    rows = line_ref.shape[1]
    here = lax.axis_index("ka") // NX
    for pair in range(pairs):
        mine_ref[pair] = line_ref[pair * parts + here]
    start = 0
    for pair, skip in PAIRS:
        for part in range(skip, parts):
            stage[start : start + rows] = line_ref[pair * parts + part].astype(F32)
            start += rows
    values = stage[...].astype(BF16)
    for copy in range(out_ref.shape[0]):
        out_ref[copy] = values


def spread_line(line):
    members, rows, _ = line.shape
    parts = members // (NB // 2)
    height = sum(parts - skip for _, skip in PAIRS) * rows
    return pl.pallas_call(
        line_kernel,
        in_specs=[VMEM],
        out_specs=[VMEM, VMEM],
        out_shape=[
            jax.ShapeDtypeStruct((NX, height, R), BF16),
            jax.ShapeDtypeStruct((NB // 2, rows, R), BF16),
        ],
        scratch_shapes=[pltpu.VMEM((height, R), F32)],
        compiler_params=pltpu.CompilerParams(vmem_limit_bytes=16 << 20),
        name="spread_line",
    )(line)


def place_rows(source, full, parity, width):
    columns = source.shape[0]
    parts = LB // (columns * width)
    values = [source[column].astype(F32) for column in range(columns)]
    start = 0
    for pair, skip in PAIRS:
        for kind in range(2):
            pieces = []
            for part in range(skip, parts):
                row = start + ((part - skip) * 2 + kind) * width
                pieces += [values[column][row : row + width] for column in range(columns)]
            rows = jnp.concatenate(pieces, axis=0).astype(BF16)
            if skip == 0:
                full[kind, 2 * pair + parity - LOW] = rows
            else:
                @pl.when(parity == 1)
                def _():
                    full[kind, 0, skip * columns * width :] = rows
                    full[kind, 0, : skip * columns * width] = jnp.zeros((skip * columns * width, R), BF16)
        start += (parts - skip) * 2 * width


def order_kernel(own_ref, full_ref):
    place_rows(own_ref, full_ref, lax.axis_index("band") % 2, LB // (lax.axis_size("ka")))


def order(own):
    return pl.pallas_call(
        order_kernel,
        in_specs=[VMEM],
        out_specs=VMEM,
        out_shape=jax.ShapeDtypeStruct((2, FULL, LB, R), BF16),
        compiler_params=pltpu.CompilerParams(vmem_limit_bytes=16 << 20),
        cost_estimate=pl.CostEstimate(flops=4 << 20, bytes_accessed=2 << 20, transcendentals=0),
        name="order",
    )(own)


def tile_kernel(tiles_ref, mine_ref, theirs_ref, own_ref, other_ref, scale_ref, out_ref, first32, full, slab_t, pair, held, sems):
    core = lax.axis_index("band") % 2
    width = mine_ref.shape[1] // 2
    row_offset = lax.axis_index("ka") * width
    slots = held.shape[0]

    def send(slot):
        return pltpu.make_async_copy(held.at[slot], out_ref.at[slot], sems.at[slot])

    for parity, source in ((core, mine_ref), (1 - core, theirs_ref)):
        for couple in range(NB // 2):
            first32[2 * couple + parity] = source[couple].astype(F32)
    for kind in range(2):
        for couple in (2, 3):
            full[kind, 2 * couple + core - LOW] = own_ref[kind, 2 * couple + core - LOW]

        @pl.when(core == 1)
        def _():
            full[kind, 0] = own_ref[kind, 0]

    place_rows(other_ref, full, 1 - core, width)
    scale = scale_ref[...] * (0.5 / math.sqrt(R))
    for kind in range(2):
        slab_t[1 - kind] = (full[kind, FULL - 1].astype(F32) * scale).T.astype(BF16)

    def one_slot(slot, carry):
        one = tiles_ref[0, slot]
        two = tiles_ref[1, slot]
        live = (one >= 0) & (one + two >= NB - LOW)

        @pl.when(live)
        def _():
            block = two - LOW
            for row in range(width):
                alpha_one = jnp.broadcast_to(first32[one, pl.ds(row, 1), :], (LB, R)).astype(BF16)
                beta_one = jnp.broadcast_to(first32[one, pl.ds(width + row, 1), :], (LB, R)).astype(BF16)
                alpha_two = full[0, block]
                beta_two = full[1, block]
                where = pl.ds(row * LB, LB)
                pair[where, :R] = alpha_one * beta_two + beta_one * alpha_two
                pair[where, R:] = beta_one * beta_two
            values = jnp.dot(pair[...], slab_t[...].reshape(2 * R, LB), preferred_element_type=F32)
            second = lax.broadcasted_iota(jnp.int32, (LB, LB), 0) + two * LB
            third = lax.broadcasted_iota(jnp.int32, (LB, LB), 1) + (NB - 1) * LB
            gap = third - second - 2
            floor = [jnp.where((second <= third) & (gap % 2 == odd), gap, NB * LB) for odd in (0, 1)]
            for row in range(width):
                first = one * LB + row_offset + row
                keep = (first >= floor[row % 2]) & (first <= second)
                held[slot, row] = jnp.where(keep, values[row * LB : (row + 1) * LB], 0.0).astype(BF16)

        @pl.when(jnp.logical_not(live))
        def _():
            held[slot] = jnp.zeros(held.shape[1:], BF16)

        send(slot).start()
        return carry

    lax.fori_loop(0, slots, one_slot, 0)
    for slot in range(slots):
        send(slot).wait()


def tiles(tile_list, mine, theirs, own, other, scale):
    slots = tile_list.shape[0]
    width = mine.shape[1] // 2
    shape = (slots, width, LB, LB)
    return pl.pallas_call(
        tile_kernel,
        in_specs=[SMEM, VMEM, VMEM, VMEM, VMEM, VMEM],
        out_specs=HBM,
        out_shape=jax.ShapeDtypeStruct(shape, BF16),
        scratch_shapes=[
            pltpu.VMEM((NB, 2 * width, R), F32),
            pltpu.VMEM((2, FULL, LB, R), BF16),
            pltpu.VMEM((2, R, LB), BF16),
            pltpu.VMEM((width * LB, 2 * R), BF16),
            pltpu.VMEM(shape, BF16),
            pltpu.SemaphoreType.DMA((slots,)),
        ],
        compiler_params=pltpu.CompilerParams(vmem_limit_bytes=40 << 20),
        name="tiles",
    )(tile_list.T, mine, theirs, own, other, scale)


def body(transfer, bessel_table, k_weight, power_spectrum, radial_weight, tile_list):
    bands = lax.axis_size("band")
    members = lax.axis_size("ka")
    depth = members // NX
    along_x = [[z * NX + x for x in range(NX)] for z in range(depth)]
    along_yz = [
        [(y * 2 + core) * members + z * NX + x for y in range(bands // 2) for z in range(depth)]
        for core in range(2)
        for x in range(NX)
    ]
    sibling = [(i, i ^ 1) for i in range(bands)]

    partial = project(transfer, k_weight, power_spectrum, bessel_table, members)
    shares = lax.all_to_all(partial, "ka", 0, 0, tiled=True)
    copies = total(shares, len(along_yz[0]))
    line = lax.all_to_all(copies, ("band", "ka"), 0, 0, axis_index_groups=along_yz, tiled=True)
    copies, mine = spread_line(line)
    theirs = lax.ppermute(mine, "band", sibling)
    own = lax.all_to_all(copies, "ka", 0, 0, axis_index_groups=along_x, tiled=True)
    other = lax.ppermute(own, "band", sibling)
    return tiles(tile_list, mine, theirs, order(own), other, radial_weight[None, :])


def solution(mesh):
    return jax.shard_map(
        body,
        mesh=mesh,
        in_specs=(P("band", "ka"), P("band", "ka", None), P("ka"), P("ka"), P(), P("band", None)),
        out_specs=P("band", "ka", None, None),
        check_vma=False,
    )
```
